32 devices in a mesh: grp: 2 (over x), rows: 16 (over z, y, core).
Axes of the slice: x: 2, y: 2, z: 4, core: 2. Of those that a mesh axis runs over, the one named last changes fastest.
Arguments:
- train_act: bfloat16 [1, 1024, 7, 7, 512], P(None, ('grp', 'rows')), parts along dimension 1, may hold values from -6 to 6
- train_grad: bfloat16 [1, 1024, 7, 7, 512], P(None, ('grp', 'rows')), parts along dimension 1, may hold values from -6 to 6
- test_act: bfloat16 [1, 32, 7, 7, 512], P(None, ('grp', 'rows')), parts along dimension 1, may hold values from -6 to 6
- test_grad: bfloat16 [1, 32, 7, 7, 512], P(None, ('grp', 'rows')), parts along dimension 1, may hold values from -6 to 6
- ckpt_weights: float32 [1], replicated, may hold values from 0.5 to 2
- owner_ids: int32 [1024, 1], P(('grp', 'rows')), parts along dimension 0, may hold values from 0 to 15; in each aligned block of 32 rows (0 to 31, 32 to 63, ...) at most 2 rows name the same one
Outputs:
- influence: float32 [1024, 16], P(('grp', 'rows')), parts along dimension 0
- owner_scores: float32 [32, 16], P(('grp', 'rows')), parts along dimension 0
The draws below stay inside these ranges and needn't reach their ends.
There are 2 independent parts, one for each index of `grp`. The reference program is written for one: setup_inputs(seed, part) draws one part's arguments, and reference() takes and returns one part's arrays. A program takes and returns all parts, laid end to end along the dimension named above; an argument that names none is the same for every part. Nothing has to cross between parts.
Inputs may be any that keep to these rules, and one draw needn't show every extreme that they name: `owner_ids`: among the training examples of one device, no owner appears more than 2 times, and some owner appears exactly 2 times.
All inputs are finite; a program needn't handle non-finite values.
Results may differ from the reference program's by a relative error of at most 0.0003.
Values may be sent and summed in bfloat16 or wider, within the bound.
No kernel may reach another device: no remote copies, remote signals or barrier semaphores. Data moves between devices by JAX's collectives and lax.ppermute only.
A program may use at most 256 MiB of HBM per device.

```python
import math
import jax
import jax.numpy as jnp
import numpy as np
from jax import lax

C = 512
S = 7
TR_DEV = 32
CKPTS = 1
CAP = 2
TRAIN = 512
TEST = 16
OWNERS = 16


def level_of(stream_key, shape, cuts, low, largest):
    loudness = 1.0
    for axis_at, blocks in cuts:
        draws = jax.random.uniform(jax.random.fold_in(jax.random.fold_in(stream_key, 6), axis_at), (blocks,), jnp.float32, low / len(cuts), largest / len(cuts))
        loudness = loudness * jnp.repeat(jnp.exp(draws), shape[axis_at] // blocks).reshape((-1,) + (1,) * (len(shape) - 1 - axis_at))
    return loudness


def shared_out(own_key, own, number, rows, number_of, top, bound, lean):
    ranking = jax.random.permutation(own_key, number_of)
    packed, usual = portions_of(number_of, rows * top, bound, lean, True), portions_of(number_of, rows * top, bound, lean, False)
    places = jnp.arange(number_of)

    def named(lengths, rotation):
        used = int((lengths > 0).sum())
        fixed = max(1, used // 4)
        moved = fixed + (places - fixed + rotation * (used - fixed)) % max(1, number_of - fixed)
        return jnp.zeros((number_of,), jnp.int32).at[ranking[jnp.where(places < fixed, places, moved)]].set(jnp.asarray(lengths, jnp.int32))

    lengths = jnp.where(number % 4 == 0, named(packed, number // 4), named(usual, number - number // 4 - 1))
    mixed = jax.random.permutation(jax.random.fold_in(own, 3), number_of)
    donor, taker = mixed[0:number_of // 2 * 2:2], mixed[1:number_of // 2 * 2:2]
    room = jnp.minimum(lengths[donor] - 1, bound - lengths[taker]) // 2
    room = jnp.where((donor == ranking[0]) | (taker == ranking[0]) | (lengths[taker] == 0), 0, jnp.maximum(room, 0))
    moved = jax.random.randint(jax.random.fold_in(own, 4), (number_of // 2,), 0, 1 << 20) % (room + 1)
    lengths = lengths.at[donor].add(-moved).at[taker].add(moved)
    items = jnp.searchsorted(jnp.cumsum(lengths), jnp.arange(rows * top), side="right").astype(jnp.int32)
    listing = items.reshape(top, rows).T
    listing = listing[jax.random.permutation(jax.random.fold_in(own, 1), rows)]
    rotation = jax.random.randint(jax.random.fold_in(own, 2), (rows, 1), 0, top)
    return jnp.take_along_axis(listing, (jnp.arange(top)[None, :] + rotation) % top, axis=1)


def portions_of(number_of, total, limit, skew, full):
    loads = [(1 << 20) // math.isqrt(grade ** skew) + 1 for grade in range(1, number_of + 1)]
    largest = limit if full else min(limit, max(-(-total // number_of), total * loads[0] // sum(loads)))
    least = 1 if total - largest >= number_of - 1 else 0
    counts, rest = [largest] + [least] * (number_of - 1), total - largest - least * (number_of - 1)
    while rest > 0:
        free = [i for i in range(1, number_of) if counts[i] < largest] or [i for i in range(1, number_of) if counts[i] < limit]
        whole, left = sum([loads[i] for i in free]), rest
        for i in free:
            more = min(limit - counts[i], max(1, left * loads[i] // whole), rest)
            counts[i] = counts[i] + more
            rest = rest - more
    return np.array(counts)


def bell_draw(key, shape, spread, reach, split=(), held_as=jnp.bfloat16):
    loudness = level_of(key, shape, split, -0.22, 0.18) if split else 1.0
    entries = jax.random.normal(key, shape, jnp.float32) * spread * loudness
    return jnp.minimum(jnp.maximum(entries, -reach), reach).astype(held_as)


def setup_inputs(seed: int = 0, part: int = 0) -> dict:
    key_of = jax.random.split(jax.random.key(seed), 7)
    part_splits = jax.random.split(jax.random.fold_in(key_of[6], part), 7)
    train_act = bell_draw(part_splits[0], (CKPTS, TRAIN, S, S, C), 1.0, 6.0, ((1, 16),))
    train_grad = bell_draw(part_splits[1], (CKPTS, TRAIN, S, S, C), 1.0, 6.0, ((1, 16),))
    test_act = bell_draw(part_splits[2], (CKPTS, TEST, S, S, C), 1.0, 6.0, ((1, 16),))
    test_grad = bell_draw(part_splits[3], (CKPTS, TEST, S, S, C), 1.0, 6.0, ((1, 16),))
    ckpt_weights = jnp.clip(jnp.exp(jax.random.uniform(key_of[4], (CKPTS,), jnp.float32, math.log(0.5), math.log(2.0))), 0.5, 2.0)
    owner_ids_keys = jax.random.split(jax.random.fold_in(part_splits[5], 1), TRAIN // TR_DEV)
    owner_ids_turns = jax.random.permutation(jax.random.fold_in(part_splits[5], 3), TRAIN // TR_DEV)
    owner_ids = jax.vmap(lambda own, number: shared_out(jax.random.fold_in(part_splits[5], 2), own, number, TR_DEV, OWNERS, 1, CAP, 2))(owner_ids_keys, owner_ids_turns).reshape((TRAIN, 1))
    return {"train_act": train_act, "train_grad": train_grad, "test_act": test_act, "test_grad": test_grad, "ckpt_weights": ckpt_weights, "owner_ids": owner_ids}


def patch_sum(gram_raw):
    extent = gram_raw.shape[1]
    padded = jnp.pad(gram_raw, ((0, 0), (1, 1), (1, 1), (0, 0), (1, 1), (1, 1)))
    summed = jnp.zeros(gram_raw.shape, gram_raw.dtype)
    for shift_y in range(3):
        for shift_x in range(3):
            summed = summed + padded[:, shift_y:shift_y + extent, shift_x:shift_x + extent, :, shift_y:shift_y + extent, shift_x:shift_x + extent]
    return summed


def pair_scores(tr_act, tr_grad, te_act, te_grad):
    rows_a = tr_act.shape[0]
    extent = tr_act.shape[1]
    channels = tr_act.shape[3]
    rows_b = te_act.shape[0]
    gram_raw = jnp.dot(tr_act.reshape(-1, channels), te_act.reshape(-1, channels).T, preferred_element_type=jnp.float32)
    gram_raw = gram_raw.reshape(rows_a, extent, extent, rows_b, extent, extent)
    grad_gram = jnp.dot(tr_grad.reshape(-1, channels), te_grad.reshape(-1, channels).T, preferred_element_type=jnp.float32)
    grad_gram = grad_gram.reshape(rows_a, extent, extent, rows_b, extent, extent)
    kernel = patch_sum(gram_raw)
    return jnp.sum(kernel * grad_gram, axis=(1, 2, 4, 5)) / (3.0 * extent * extent * channels)


def reference(train_act, train_grad, test_act, test_grad, ckpt_weights, owner_ids):
    def one_test(position):
        summed = jnp.zeros((TRAIN,), jnp.float32)
        for checkpoint in range(CKPTS):
            test_acts = lax.dynamic_slice_in_dim(test_act[checkpoint], position, 1, 0)
            test_grads = lax.dynamic_slice_in_dim(test_grad[checkpoint], position, 1, 0)
            summed = summed + ckpt_weights[checkpoint] * pair_scores(train_act[checkpoint], train_grad[checkpoint], test_acts, test_grads)[:, 0]
        return summed

    columns = lax.map(one_test, jnp.arange(TEST, dtype=jnp.int32))
    influence = columns.T
    onehot = (owner_ids[:, 0][None, :] == jnp.arange(OWNERS, dtype=jnp.int32)[:, None]).astype(jnp.float32)
    owner_scores = jnp.dot(onehot, influence, precision=lax.Precision.HIGHEST)
    return influence, owner_scores
```

```python
import functools

import jax
import jax.numpy as jnp
from jax import lax
from jax.experimental import pallas as pl
from jax.experimental.pallas import tpu as pltpu
from jax.sharding import PartitionSpec as P

CHUNK = 4
LANES = 64
HIGHEST = lax.Precision.HIGHEST


def nt_dot(a, b, precision=None):
    return lax.dot_general(
        a, b, (((1,), (1,)), ((), ())), precision=precision, preferred_element_type=jnp.float32
    )


def pack_test(act, grad):
    side, channels = act.shape[0], act.shape[2]
    act = jnp.pad(act, ((0, 0), (0, 8 - side), (0, 0)))
    grad = jnp.pad(grad, ((0, 0), (0, 8 - side), (0, 0)))
    pieces = (act[: side - 1], grad[: side - 1], act[side - 1 :], grad[side - 1 :])
    return jnp.concatenate([piece.reshape(-1, channels) for piece in pieces], axis=0)


def chunk_kernel(base, last, side, scale, chip_ref, weight_ref, ids_ref, prev_ref, *refs):
    tests = refs[:CHUNK]
    train_act = refs[CHUNK : CHUNK + 2]
    train_grad = refs[CHUNK + 2 : CHUNK + 4]
    outs = refs[CHUNK + 4 : CHUNK + 6 if last else CHUNK + 5]
    act_w, grad_w, raw, gram = refs[-4:]
    head = (side - 1) * 8
    channels = act_w.shape[1]
    for t in range(CHUNK):
        act_w[t * LANES : t * LANES + head] = tests[t][:head]
        grad_w[t * LANES : t * LANES + head] = tests[t][head : 2 * head]
        tail = tests[t][2 * head : 2 * head + 16].astype(jnp.float32)
        blank = jnp.zeros((8, channels), jnp.float32)
        act_w[t * LANES + head : (t + 1) * LANES] = jnp.concatenate([tail[:8], blank]).astype(
            jnp.bfloat16
        )
        grad_w[t * LANES + head : (t + 1) * LANES] = jnp.concatenate([tail[8:], blank]).astype(
            jnp.bfloat16
        )

    chips = prev_ref.shape[1]
    rows = train_act[0].shape[0] // (side * side)
    line = side * rows
    lanes = CHUNK * LANES
    tested = lax.broadcasted_iota(jnp.int32, (chips, lanes), 0) ^ chip_ref[0]
    holds = lax.broadcasted_iota(jnp.int32, (chips, lanes), 1) // LANES + base
    chosen = (tested == holds).astype(jnp.float32)

    scores = []
    for half in range(2):
        for a in range(side):
            cut = slice(a * line, (a + 1) * line)
            raw[half, cut] = nt_dot(train_act[half][cut], act_w[...])
            gram[half, cut] = nt_dot(train_grad[half][cut], grad_w[...])
        totals = []
        for lane in range(0, lanes, 128):
            total = jnp.zeros((rows, 128), jnp.float32)
            for a in range(side):
                columns = []
                for b in range(side):
                    at = (a * side + b) * rows
                    column = raw[half, at : at + rows, lane : lane + 128]
                    if a > 0:
                        column += pltpu.roll(
                            raw[half, at - line : at - line + rows, lane : lane + 128], 8, 1
                        )
                    if a < side - 1:
                        column += pltpu.roll(
                            raw[half, at + line : at + line + rows, lane : lane + 128], 120, 1
                        )
                    columns.append(column)
                for b in range(side):
                    at = (a * side + b) * rows
                    patch = columns[b]
                    if b > 0:
                        patch += pltpu.roll(columns[b - 1], 1, 1)
                    if b < side - 1:
                        patch += pltpu.roll(columns[b + 1], 127, 1)
                    total += patch * gram[half, at : at + rows, lane : lane + 128]
            totals.append(total)
        scores.append(nt_dot(chosen, jnp.concatenate(totals, axis=1), HIGHEST) + prev_ref[half])
    if not last:
        for half in range(2):
            outs[0][half] = scores[half]
        return
    owned = 0.0
    for half in range(2):
        influence = scores[half] * (weight_ref[0] * scale)
        outs[0][half] = influence
        number_of = outs[1].shape[0]
        owner = lax.broadcasted_iota(jnp.int32, (number_of, rows), 0)
        hit = (owner == ids_ref[half : half + 1]).astype(jnp.float32)
        owned += nt_dot(hit, influence, HIGHEST)
    outs[1][...] = owned


def chunk_scores(base, last, side, owners, scale, chip, weight, ids, prev, tests, acts, grads):
    rows, channels = acts[0].shape
    lanes = CHUNK * LANES
    out_shape = [jax.ShapeDtypeStruct(prev.shape, jnp.float32)]
    if last:
        out_shape.append(jax.ShapeDtypeStruct((owners, prev.shape[1]), jnp.float32))
    vmem, smem = pl.BlockSpec(memory_space=pltpu.VMEM), pl.BlockSpec(memory_space=pltpu.SMEM)
    return pl.pallas_call(
        functools.partial(chunk_kernel, base, last, side, scale),
        out_shape=out_shape,
        in_specs=[smem, smem] + [vmem] * (2 + CHUNK + 4),
        out_specs=[vmem] * len(out_shape),
        scratch_shapes=[
            pltpu.VMEM((lanes, channels), jnp.bfloat16),
            pltpu.VMEM((lanes, channels), jnp.bfloat16),
            pltpu.VMEM((2, rows, lanes), jnp.float32),
            pltpu.VMEM((2, rows, lanes), jnp.float32),
        ],
        compiler_params=pltpu.CompilerParams(vmem_limit_bytes=48 * 1024 * 1024),
        cost_estimate=pl.CostEstimate(
            flops=8 * rows * lanes * channels, bytes_accessed=8 * rows * channels, transcendentals=0
        ),
        name="chunk_scores",
    )(chip, weight, ids, prev, *tests, *acts, *grads)


def across(x, distance):
    size = lax.axis_size("rows")
    return lax.ppermute(x, "rows", [(i, i ^ distance) for i in range(size)])


def gather_tests(own):
    chips = lax.axis_size("rows") // 2
    held = {0: own}
    if chips == 8:
        held[4] = across(own, 8)
        held[6] = across(own, 12)
        held[2] = across(own, 4)
        held[1] = across(own, 2)
        held[3] = across(own, 6)
        held[5] = across(held[4], 2)
        held[7] = across(held[6], 2)
        return held
    bit = 1
    while bit < chips:
        for known in list(held):
            held[known ^ bit] = across(held[known], 2 * bit)
        bit *= 2
    return held


def body(train_act, train_grad, test_act, test_grad, ckpt_weights, owner_ids):
    tr_dev, side, channels = train_act.shape[1], train_act.shape[2], train_act.shape[4]
    size = lax.axis_size("rows")
    chips = size // 2
    me = lax.axis_index("rows")
    held = gather_tests(pack_test(test_act[0, 0], test_grad[0, 0]))

    own_act = train_act[0].transpose(1, 2, 0, 3).reshape(-1, channels)
    own_grad = train_grad[0].transpose(1, 2, 0, 3).reshape(-1, channels)
    acts = (own_act, across(own_act, 1))
    grads = (own_grad, across(own_grad, 1))
    own_ids = owner_ids.reshape(1, tr_dev)
    ids = jnp.concatenate([own_ids, across(own_ids, 1)], axis=0)

    chip = (me // 2).reshape(1)
    scale = 1.0 / (3.0 * side * side * channels)
    scores = jnp.zeros((2, chips, tr_dev), jnp.float32)
    for base in range(0, chips, CHUNK):
        last = base + CHUNK >= chips
        tests = [held[base + t] for t in range(CHUNK)]
        done = chunk_scores(
            base, last, side, size, scale, chip, ckpt_weights, ids, scores, tests, acts, grads
        )
        scores = done[0]
    mine, packed = scores[0], done[1]

    other = across(scores[1], 1)
    received = lax.all_to_all(packed, "rows", split_axis=0, concat_axis=0, tiled=True)
    core = lax.broadcasted_iota(jnp.int32, (1, 2, 1), 1)
    influence = jnp.where(core == me % 2, mine[:, None, :], other[:, None, :]).reshape(size, tr_dev)
    totals = jnp.sum(received.reshape(chips, 2, chips), axis=0)
    return influence.T, totals.T.reshape(1, size)


def solution(mesh):
    placed = (
        P(None, ("grp", "rows"), None, None, None),
        P(None, ("grp", "rows"), None, None, None),
        P(None, ("grp", "rows"), None, None, None),
        P(None, ("grp", "rows"), None, None, None),
        P(),
        P(("grp", "rows"), None),
    )
    return jax.shard_map(
        body,
        mesh=mesh,
        in_specs=placed,
        out_specs=(P(("grp", "rows"), None), P(("grp", "rows"), None)),
        check_vma=False,
    )
```

```python
import functools

import jax
import jax.numpy as jnp
from jax import lax
from jax.experimental import pallas as pl
from jax.experimental.pallas import tpu as pltpu
from jax.sharding import PartitionSpec as P

CHUNK = 4
HIGHEST = lax.Precision.HIGHEST


def nt_dot(a, b, precision=None):
    return lax.dot_general(
        a, b, (((1,), (1,)), ((), ())), precision=precision, preferred_element_type=jnp.float32
    )


def pack_test(act, grad):
    side, channels = act.shape[0], act.shape[2]
    maps = jnp.stack([act, grad])
    return jnp.pad(maps, ((0, 0), (0, 0), (0, 8 - side), (0, 0))).reshape(-1, channels)


def chunk_kernel(distances, first, last, side, scale, me_ref, *refs):
    number = len(distances)
    if not first:
        prev_ref, refs = refs[0], refs[1:]
    if last:
        weight_ref, ids, refs = refs[0], refs[1:3], refs[3:]
    tests, refs = refs[:number], refs[number:]
    train_act, train_grad, score_ref, refs = refs[:2], refs[2:4], refs[4], refs[5:]
    act_w, grad_w, raw, part, gram, sems = refs[-6:]
    if first:
        copies = [
            pltpu.make_async_copy(pair[1], kept, sems.at[k])
            for k, (pair, kept) in enumerate(zip((train_act, train_grad), refs))
        ]
        for copy in copies:
            copy.start()
        train_act, train_grad = (train_act[0], refs[0]), (train_grad[0], refs[1])
    head = (side - 1) * 8
    channels = act_w.shape[1]
    rows = train_act[0].shape[0] // (side * side)
    folds = 128 // (2 * rows)
    steps = 8 // folds

    seams = [tests[t][head : head + 16].astype(jnp.float32) for t in range(number)]
    for t in range(number):
        act_w[t * head : (t + 1) * head] = tests[t][:head]
        grad_w[t * head : (t + 1) * head] = tests[t][head + 16 :]
    act_seam = jnp.concatenate([seam[:8] for seam in seams], axis=0)
    grad_seam = jnp.concatenate([seam[8:] for seam in seams], axis=0)
    act_w[number * head :] = act_seam.astype(jnp.bfloat16)
    grad_w[number * head :] = grad_seam.astype(jnp.bfloat16)

    def at(t, u):
        start = t * head + u * 8 if u < side - 1 else number * head + t * 8
        return slice(start, start + 8)

    def grad_at(t, u):
        start = t * head + (u - 1) * 8 if u > 0 else number * head + t * 8
        return slice(start, start + 8)

    def trains(pair, block):
        a, b = divmod(block, side)
        pieces = []
        for fold in range(folds):
            place = ((a + fold * steps) * side + b) * rows
            if a + fold * steps < side:
                pieces += [half[place : place + rows] for half in pair]
            else:
                pieces.append(jnp.zeros((2 * rows, channels), jnp.bfloat16))
        return pieces

    def products(left, pair, out, block):
        both = jnp.concatenate(trains(pair, block) + trains(pair, block + 1), axis=0)
        got = nt_dot(left[...], both)
        out[block] = got[:, :128]
        out[block + 1] = got[:, 128:]

    def neighbour(a, b, shift, place):
        if 0 <= a + shift < steps:
            return raw[(a + shift) * side + b, place]
        wrapped = raw[((a + shift) % steps) * side + b, place]
        return pltpu.roll(wrapped, 128 - 2 * rows if shift > 0 else 2 * rows, 1)

    blocks = steps * side
    if first:
        copies[0].wait()
    for block in range(0, blocks, 2):
        products(act_w, train_act, raw, block)
    for a in range(steps):
        for b in range(side):
            for t in range(number):
                for u in range(side):
                    column = raw[a * side + b, at(t, u)]
                    if u < side - 1:
                        column += neighbour(a, b, 1, at(t, u + 1))
                    if u > 0:
                        column += neighbour(a, b, -1, at(t, u - 1))
                    part[a * side + b, at(t, u)] = column
    if first:
        copies[1].wait()
    totals = [jnp.zeros((8, 128), jnp.float32) for _ in range(number)]
    for block in range(0, blocks, 2):
        products(grad_w, train_grad, gram, block)
        for one in (block, block + 1):
            b = one % side
            for t in range(number):
                for u in range(side):
                    patch = part[one, at(t, u)]
                    if b < side - 1:
                        patch += pltpu.roll(part[one + 1, at(t, u)], 7, 0)
                    if b > 0:
                        patch += pltpu.roll(part[one - 1, at(t, u)], 1, 0)
                    totals[t] += patch * gram[one, grad_at(t, u)]

    tested = lax.broadcasted_iota(jnp.int32, score_ref.shape, 0) ^ me_ref[0]
    scores = jnp.zeros(score_ref.shape, jnp.float32) if first else prev_ref[...]
    for t in range(number):
        summed = jnp.sum(totals[t], axis=0, keepdims=True)
        score = summed
        for fold in range(1, folds):
            score += pltpu.roll(summed, 2 * rows * fold, 1)
        scores += jnp.where(tested == distances[t], score, 0.0)
    if not last:
        score_ref[...] = scores
        return
    influence = scores * (weight_ref[0] * scale)
    score_ref[...] = influence
    owned_ref = refs[0]
    owner = lax.broadcasted_iota(jnp.int32, (owned_ref.shape[0], rows), 0)
    owned = 0.0
    for half in range(2):
        hit = (owner == ids[half][...]).astype(jnp.float32)
        owned += nt_dot(hit, influence[:, half * rows : (half + 1) * rows], HIGHEST)
    owned_ref[...] = owned


def chunk_scores(distances, last, side, size, scale, me, weight, ids, prev, tests, acts, grads):
    first = prev is None
    rows, channels = acts[0].shape
    number = len(distances)
    height = number * side * 8
    folds = 128 // (2 * rows // (side * side))
    blocks = 8 // folds * side
    out_shape = [jax.ShapeDtypeStruct((size, 128), jnp.float32)]
    vmem, smem = pl.BlockSpec(memory_space=pltpu.VMEM), pl.BlockSpec(memory_space=pltpu.SMEM)
    args, in_specs = [me], [smem]
    if not first:
        args, in_specs = args + [prev], in_specs + [vmem]
    if last:
        args, in_specs = args + [weight, *ids], in_specs + [smem, vmem, vmem]
        out_shape.append(jax.ShapeDtypeStruct((size, size), jnp.float32))
    partner = vmem
    if first:
        out_shape += [jax.ShapeDtypeStruct((rows, channels), jnp.bfloat16)] * 2
        partner = pl.BlockSpec(memory_space=pl.ANY)
    args += [*tests, *acts, *grads]
    in_specs += [vmem] * number + [vmem, partner] * 2
    return pl.pallas_call(
        functools.partial(chunk_kernel, distances, first, last, side, scale),
        out_shape=out_shape,
        in_specs=in_specs,
        out_specs=[vmem] * len(out_shape),
        scratch_shapes=[
            pltpu.VMEM((height, channels), jnp.bfloat16),
            pltpu.VMEM((height, channels), jnp.bfloat16),
            pltpu.VMEM((blocks, height, 128), jnp.float32),
            pltpu.VMEM((blocks, height, 128), jnp.float32),
            pltpu.VMEM((blocks, height, 128), jnp.float32),
            pltpu.SemaphoreType.DMA((2,)),
        ],
        compiler_params=pltpu.CompilerParams(vmem_limit_bytes=16 * 1024 * 1024),
        cost_estimate=pl.CostEstimate(
            flops=4 * blocks * 128 * height * channels, bytes_accessed=0, transcendentals=0
        ),
        name="chunk_scores",
    )(*args)


def later_kernel(ids_ref, test_ref, out_ref):
    out_ref[...] = test_ref[...]


def after(test, ids):
    vmem = pl.BlockSpec(memory_space=pltpu.VMEM)
    return pl.pallas_call(
        later_kernel,
        out_shape=jax.ShapeDtypeStruct(test.shape, test.dtype),
        in_specs=[vmem, vmem],
        out_specs=vmem,
        compiler_params=pltpu.CompilerParams(vmem_limit_bytes=1024 * 1024),
        cost_estimate=pl.CostEstimate(flops=8_000_000_000, bytes_accessed=0, transcendentals=0),
        name="after",
    )(ids, test)


def across(x, distance):
    size = lax.axis_size("rows")
    return lax.ppermute(x, "rows", [(i, i ^ distance) for i in range(size)])


def gather_tests(own, later):
    size = lax.axis_size("rows")
    held = {0: own}
    if size == 16:
        held[8] = across(own, 8)
        held[4] = across(later, 4)
        held[2] = across(later, 2)
        held[14] = across(held[8], 6)
        held[12] = across(held[8], 4)
        held[10] = across(held[8], 2)
        held[6] = across(held[4], 2)
        return held, [[0, 8, 4, 2], [6, 10, 12, 14]]
    bit = 2
    while bit < size:
        for known in list(held):
            held[known ^ bit] = across(held[known], bit)
        bit *= 2
    known = sorted(held)
    return held, [known[i : i + CHUNK] for i in range(0, len(known), CHUNK)]


def body(train_act, train_grad, test_act, test_grad, ckpt_weights, owner_ids):
    tr_dev, side, channels = train_act.shape[1], train_act.shape[2], train_act.shape[4]
    size = lax.axis_size("rows")
    own_act = train_act[0].transpose(1, 2, 0, 3).reshape(-1, channels)
    own_grad = train_grad[0].transpose(1, 2, 0, 3).reshape(-1, channels)
    own_ids = owner_ids.reshape(1, tr_dev)
    ids = (own_ids, across(own_ids, 1))
    acts, grads = (own_act, across(own_act, 1)), (own_grad, across(own_grad, 1))

    own_test = pack_test(test_act[0, 0], test_grad[0, 0])
    later = after(own_test, ids[1])
    held, chunks = gather_tests(own_test, later)

    me = lax.axis_index("rows").reshape(1)
    scale = 1.0 / (3.0 * side * side * channels)
    done = [None]
    for k, distances in enumerate(chunks):
        last = k == len(chunks) - 1
        tests = [held[distance] for distance in distances]
        done = chunk_scores(
            distances, last, side, size, scale, me, ckpt_weights, ids, done[0], tests, acts, grads
        )
        if k == 0:
            acts, grads = (acts[0], done[1]), (grads[0], done[2])
    scores, packed = done

    received = lax.all_to_all(packed, "rows", split_axis=0, concat_axis=0, tiled=True)
    influence = scores[:, :tr_dev] + across(scores[:, tr_dev : 2 * tr_dev], 1)
    return influence.T, jnp.sum(received, axis=0, keepdims=True)


def solution(mesh):
    placed = (
        P(None, ("grp", "rows"), None, None, None),
        P(None, ("grp", "rows"), None, None, None),
        P(None, ("grp", "rows"), None, None, None),
        P(None, ("grp", "rows"), None, None, None),
        P(),
        P(("grp", "rows"), None),
    )
    return jax.shard_map(
        body,
        mesh=mesh,
        in_specs=placed,
        out_specs=(P(("grp", "rows"), None), P(("grp", "rows"), None)),
        check_vma=False,
    )
```

```python
import functools

import jax
import jax.numpy as jnp
from jax import lax
from jax.experimental import pallas as pl
from jax.experimental.pallas import tpu as pltpu
from jax.sharding import PartitionSpec as P

CHUNK = 4
HIGHEST = lax.Precision.HIGHEST


def nt_dot(a, b, precision=None):
    return lax.dot_general(
        a, b, (((1,), (1,)), ((), ())), precision=precision, preferred_element_type=jnp.float32
    )


def pack_test(act, grad):
    side, channels = act.shape[0], act.shape[2]
    maps = jnp.stack([act, grad])
    return jnp.pad(maps, ((0, 0), (0, 0), (0, 8 - side), (0, 0))).reshape(-1, channels)


def chunk_kernel(distances, places, first, last, side, scale, me_ref, *refs):
    number = len(distances)
    if not first:
        prev_ref, refs = refs[0], refs[1:]
    if last:
        weight_ref, ids, refs = refs[0], refs[1], refs[2:]
    arrays = 1 + max(array for array, _ in places)
    tests, refs = refs[:arrays], refs[arrays:]
    train_act, train_grad, score_ref, refs = refs[0], refs[1], refs[2], refs[3:]
    act_w, grad_w, raw, part, gram = refs[-5:]
    head = (side - 1) * 8
    channels = act_w.shape[1]
    rows = train_act.shape[0] // (side * side)
    folds = 128 // rows
    steps = 8 // folds

    def test_rows(t, start, stop):
        array, place = places[t]
        return tests[array][place + start : place + stop]

    seams = [test_rows(t, head, head + 16).astype(jnp.float32) for t in range(number)]
    for t in range(number):
        act_w[t * head : (t + 1) * head] = test_rows(t, 0, head)
        grad_w[t * head : (t + 1) * head] = test_rows(t, head + 16, 2 * head + 16)
    act_seam = jnp.concatenate([seam[:8] for seam in seams], axis=0)
    grad_seam = jnp.concatenate([seam[8:] for seam in seams], axis=0)
    act_w[number * head :] = act_seam.astype(jnp.bfloat16)
    grad_w[number * head :] = grad_seam.astype(jnp.bfloat16)

    def at(t, u):
        start = t * head + u * 8 if u < side - 1 else number * head + t * 8
        return slice(start, start + 8)

    def grad_at(t, u):
        start = t * head + (u - 1) * 8 if u > 0 else number * head + t * 8
        return slice(start, start + 8)

    def trains(source, block):
        a, b = divmod(block, side)
        pieces = []
        for fold in range(folds):
            place = ((a + fold * steps) * side + b) * rows
            if a + fold * steps < side:
                pieces.append(source[place : place + rows])
            else:
                pieces.append(jnp.zeros((rows, channels), jnp.bfloat16))
        return pieces

    def products(left, pair, out, block):
        both = jnp.concatenate(trains(pair, block) + trains(pair, block + 1), axis=0)
        got = nt_dot(left[...], both)
        out[block] = got[:, :128]
        out[block + 1] = got[:, 128:]

    def neighbour(a, b, shift, place):
        if 0 <= a + shift < steps:
            return raw[(a + shift) * side + b, place]
        wrapped = raw[((a + shift) % steps) * side + b, place]
        return pltpu.roll(wrapped, 128 - rows if shift > 0 else rows, 1)

    blocks = steps * side
    totals = [jnp.zeros((8, 128), jnp.float32) for _ in range(number)]

    def dy_sum(a):
        for b in range(side):
            for t in range(number):
                for u in range(side):
                    column = raw[a * side + b, at(t, u)]
                    if u < side - 1:
                        column += neighbour(a, b, 1, at(t, u + 1))
                    if u > 0:
                        column += neighbour(a, b, -1, at(t, u - 1))
                    part[a * side + b, at(t, u)] = column

    def score(one):
        b = one % side
        for t in range(number):
            for u in range(side):
                patch = part[one, at(t, u)]
                if b < side - 1:
                    patch += pltpu.roll(part[one + 1, at(t, u)], 7, 0)
                if b > 0:
                    patch += pltpu.roll(part[one - 1, at(t, u)], 1, 0)
                totals[t] += patch * gram[one, grad_at(t, u)]

    raw_order = list(range(0, blocks, 2))
    grams = list(range(0, blocks, 2))
    made, summed, scored, gram_made = set(), 0, 0, 0
    for block in raw_order:
        products(act_w, train_act, raw, block)
        made |= {block, block + 1}
        while summed < steps and all(
            a % steps * side + b in made for a in (summed - 1, summed, summed + 1) for b in range(side)
        ):
            dy_sum(summed)
            summed += 1
    for block in grams:
        products(grad_w, train_grad, gram, block)
        while scored < block + 2 and (scored // side + 1) <= summed:
            score(scored)
            scored += 1
    assert summed == steps and scored == blocks

    tested = lax.broadcasted_iota(jnp.int32, score_ref.shape, 0) ^ me_ref[0]
    scores = jnp.zeros(score_ref.shape, jnp.float32) if first else prev_ref[...]
    for t in range(number):
        summed = jnp.sum(totals[t], axis=0, keepdims=True)
        score = summed
        for fold in range(1, folds):
            score += pltpu.roll(summed, rows * fold, 1)
        scores += jnp.where(tested == distances[t], score, 0.0)
    if not last:
        score_ref[...] = scores
        return
    influence = scores * (weight_ref[0] * scale)
    score_ref[...] = influence
    owned_ref = refs[0]
    owner = lax.broadcasted_iota(jnp.int32, (owned_ref.shape[0], rows), 0)
    hit = (owner == ids[...]).astype(jnp.float32)
    owned_ref[...] = nt_dot(hit, influence[:, :rows], HIGHEST)


def chunk_scores(distances, places, last, side, size, scale, me, weight, ids, prev, tests, act, grad):
    first = prev is None
    rows, channels = act.shape
    height = len(distances) * side * 8
    blocks = 8 // (128 // (rows // (side * side))) * side
    out_shape = [jax.ShapeDtypeStruct((size, 128), jnp.float32)]
    vmem, smem = pl.BlockSpec(memory_space=pltpu.VMEM), pl.BlockSpec(memory_space=pltpu.SMEM)
    args, in_specs = [me], [smem]
    if not first:
        args, in_specs = args + [prev], in_specs + [vmem]
    if last:
        args, in_specs = args + [weight, ids], in_specs + [smem, vmem]
        out_shape.append(jax.ShapeDtypeStruct((size, size), jnp.float32))
    args, in_specs = args + [*tests, act, grad], in_specs + [vmem] * (len(tests) + 2)
    return pl.pallas_call(
        functools.partial(chunk_kernel, distances, places, first, last, side, scale),
        out_shape=out_shape,
        in_specs=in_specs,
        out_specs=[vmem] * len(out_shape),
        scratch_shapes=[
            pltpu.VMEM((height, channels), jnp.bfloat16),
            pltpu.VMEM((height, channels), jnp.bfloat16),
            pltpu.VMEM((blocks, height, 128), jnp.float32),
            pltpu.VMEM((blocks, height, 128), jnp.float32),
            pltpu.VMEM((blocks, height, 128), jnp.float32),
        ],
        compiler_params=pltpu.CompilerParams(vmem_limit_bytes=24 * 1024 * 1024),
        cost_estimate=pl.CostEstimate(
            flops=4 * blocks * 128 * height * channels, bytes_accessed=0, transcendentals=0
        ),
        name="chunk_scores",
    )(*args)


def across(x, distance):
    size = lax.axis_size("rows")
    return lax.ppermute(x, "rows", [(i, i ^ distance) for i in range(size)])


def gather_tests(own):
    size, height = lax.axis_size("rows"), own.shape[0]
    held = {0: own}
    other = across(own, 1)
    if size == 16:
        later, other = lax.optimization_barrier((own, other))
        held[8] = across(own, 8)
        held[4] = across(later, 4)
        held[2] = across(later, 2)
        held[6] = across(later, 6)
        held[14] = across(held[8], 6)
        held[12] = across(held[8], 4)
        held[10] = across(held[8], 2)
        groups = [[0, 2, 4, 6], [8, 10, 12, 14]]
    else:
        bit = 2
        while bit < size:
            for known in list(held):
                held[known ^ bit] = across(held[known], bit)
            bit *= 2
        groups = [list(range(i, i + 2 * CHUNK, 2)) for i in range(0, size, 2 * CHUNK)]
    return held, other, groups


def body(train_act, train_grad, test_act, test_grad, ckpt_weights, owner_ids):
    tr_dev, side, channels = train_act.shape[1], train_act.shape[2], train_act.shape[4]
    size = lax.axis_size("rows")
    act = train_act[0].transpose(1, 2, 0, 3).reshape(-1, channels)
    grad = train_grad[0].transpose(1, 2, 0, 3).reshape(-1, channels)
    ids = owner_ids.reshape(1, tr_dev)
    held, other, groups = gather_tests(pack_test(test_act[0, 0], test_grad[0, 0]))

    me = lax.axis_index("rows").reshape(1)
    scale = 1.0 / (3.0 * side * side * channels)
    scores, came, sent_on = None, {1: other}, {}
    for k in range(len(groups) + 1):
        last, group = k == len(groups), groups[k] if k < len(groups) else []
        if k != 1 or len(groups) > 2:
            came, sent_on = came | sent_on, {}
        distances, arrays = group + list(came), [held[d] for d in group] + list(came.values())
        late = group[1:] if k else []
        if late:
            *sent, scores = lax.optimization_barrier((*[held[d] for d in late], scores))
        sent = dict(zip(late, sent)) if late else {}
        came = {}
        sent_on |= {d ^ 1: across(sent.get(d, held[d]), 1) for d in group if d}
        places = [(test, 0) for test in range(len(arrays))]
        done = chunk_scores(
            distances, places, last, side, size, scale, me, ckpt_weights, ids, scores, arrays, act, grad
        )
        scores = done[0]
    scores, packed = done
    received = lax.all_to_all(packed, "rows", split_axis=0, concat_axis=0, tiled=True)
    return scores[:, :tr_dev].T, jnp.sum(received, axis=0, keepdims=True)


def solution(mesh):
    placed = (
        P(None, ("grp", "rows"), None, None, None),
        P(None, ("grp", "rows"), None, None, None),
        P(None, ("grp", "rows"), None, None, None),
        P(None, ("grp", "rows"), None, None, None),
        P(),
        P(("grp", "rows"), None),
    )
    return jax.shard_map(
        body,
        mesh=mesh,
        in_specs=placed,
        out_specs=(P(("grp", "rows"), None), P(("grp", "rows"), None)),
        check_vma=False,
    )
```

```python
import functools

import jax
import jax.numpy as jnp
from jax import lax
from jax.experimental import pallas as pl
from jax.experimental.pallas import tpu as pltpu
from jax.sharding import PartitionSpec as P

CHUNK = 4
HIGHEST = lax.Precision.HIGHEST


def nt_dot(a, b, precision=None):
    return lax.dot_general(
        a, b, (((1,), (1,)), ((), ())), precision=precision, preferred_element_type=jnp.float32
    )


def pack_test(act, grad):
    side, channels = act.shape[0], act.shape[2]
    maps = jnp.stack([act, grad])
    return jnp.pad(maps, ((0, 0), (0, 0), (0, 8 - side), (0, 0))).reshape(-1, channels)


def chunk_kernel(distances, places, first, last, side, scale, me_ref, *refs):
    number = len(distances)
    if not first:
        prev_ref, refs = refs[0], refs[1:]
    if last:
        weight_ref, ids, refs = refs[0], refs[1], refs[2:]
    arrays = 1 + max(array for array, _ in places)
    tests, refs = refs[:arrays], refs[arrays:]
    train_act, train_grad, score_ref, refs = refs[0], refs[1], refs[2], refs[3:]
    act_w, grad_w, raw, part, gram = refs[-5:]
    head = (side - 1) * 8
    channels = act_w.shape[1]
    rows = train_act.shape[0] // (side * side)
    folds = 128 // rows
    steps = 8 // folds

    def test_rows(t, start, stop):
        array, place = places[t]
        return tests[array][place + start : place + stop]

    seams = [test_rows(t, head, head + 16).astype(jnp.float32) for t in range(number)]
    for t in range(number):
        act_w[t * head : (t + 1) * head] = test_rows(t, 0, head)
        grad_w[t * head : (t + 1) * head] = test_rows(t, head + 16, 2 * head + 16)
    act_seam = jnp.concatenate([seam[:8] for seam in seams], axis=0)
    grad_seam = jnp.concatenate([seam[8:] for seam in seams], axis=0)
    act_w[number * head :] = act_seam.astype(jnp.bfloat16)
    grad_w[number * head :] = grad_seam.astype(jnp.bfloat16)

    def at(t, u):
        start = t * head + u * 8 if u < side - 1 else number * head + t * 8
        return slice(start, start + 8)

    def grad_at(t, u):
        start = t * head + (u - 1) * 8 if u > 0 else number * head + t * 8
        return slice(start, start + 8)

    def trains(source, block):
        a, b = divmod(block, side)
        pieces = []
        for fold in range(folds):
            place = ((a + fold * steps) * side + b) * rows
            if a + fold * steps < side:
                pieces.append(source[place : place + rows])
            else:
                pieces.append(jnp.zeros((rows, channels), jnp.bfloat16))
        return pieces

    def products(left, pair, out, block):
        both = jnp.concatenate(trains(pair, block) + trains(pair, block + 1), axis=0)
        got = nt_dot(left[...], both)
        out[block] = got[:, :128]
        out[block + 1] = got[:, 128:]

    def neighbour(a, b, shift, place):
        if 0 <= a + shift < steps:
            return raw[(a + shift) * side + b, place]
        wrapped = raw[((a + shift) % steps) * side + b, place]
        return pltpu.roll(wrapped, 128 - rows if shift > 0 else rows, 1)

    blocks = steps * side
    totals = [jnp.zeros((8, 128), jnp.float32) for _ in range(number)]

    def dy_sum(a):
        for b in range(side):
            for t in range(number):
                for u in range(side):
                    column = raw[a * side + b, at(t, u)]
                    if u < side - 1:
                        column += neighbour(a, b, 1, at(t, u + 1))
                    if u > 0:
                        column += neighbour(a, b, -1, at(t, u - 1))
                    part[a * side + b, at(t, u)] = column

    def score(one):
        b = one % side
        for t in range(number):
            for u in range(side):
                patch = part[one, at(t, u)]
                if b < side - 1:
                    patch += pltpu.roll(part[one + 1, at(t, u)], 7, 0)
                if b > 0:
                    patch += pltpu.roll(part[one - 1, at(t, u)], 1, 0)
                totals[t] += patch * gram[one, grad_at(t, u)]

    raw_order = list(range(0, blocks, 2))
    grams = list(range(0, blocks, 2))
    made, summed, scored, gram_made = set(), 0, 0, 0
    for block in raw_order:
        products(act_w, train_act, raw, block)
        made |= {block, block + 1}
        while summed < steps and all(
            a % steps * side + b in made for a in (summed - 1, summed, summed + 1) for b in range(side)
        ):
            dy_sum(summed)
            summed += 1
    for block in grams:
        products(grad_w, train_grad, gram, block)
        while scored < block + 2 and (scored // side + 1) <= summed:
            score(scored)
            scored += 1
    assert summed == steps and scored == blocks

    tested = lax.broadcasted_iota(jnp.int32, score_ref.shape, 0) ^ me_ref[0]
    scores = jnp.zeros(score_ref.shape, jnp.float32) if first else prev_ref[...]
    for t in range(number):
        summed = jnp.sum(totals[t], axis=0, keepdims=True)
        score = summed
        for fold in range(1, folds):
            score += pltpu.roll(summed, rows * fold, 1)
        scores += jnp.where(tested == distances[t], score, 0.0)
    if not last:
        score_ref[...] = scores
        return
    influence = scores * (weight_ref[0] * scale)
    score_ref[...] = influence
    owned_ref = refs[0]
    owner = lax.broadcasted_iota(jnp.int32, (owned_ref.shape[0], rows), 0)
    hit = (owner == ids[...]).astype(jnp.float32)
    owned_ref[...] = nt_dot(hit, influence[:, :rows], HIGHEST)


def chunk_scores(distances, places, last, side, size, scale, me, weight, ids, prev, tests, act, grad):
    first = prev is None
    rows, channels = act.shape
    height = len(distances) * side * 8
    blocks = 8 // (128 // (rows // (side * side))) * side
    out_shape = [jax.ShapeDtypeStruct((size, 128), jnp.float32)]
    vmem, smem = pl.BlockSpec(memory_space=pltpu.VMEM), pl.BlockSpec(memory_space=pltpu.SMEM)
    args, in_specs = [me], [smem]
    if not first:
        args, in_specs = args + [prev], in_specs + [vmem]
    if last:
        args, in_specs = args + [weight, ids], in_specs + [smem, vmem]
        out_shape.append(jax.ShapeDtypeStruct((size, size), jnp.float32))
    args, in_specs = args + [*tests, act, grad], in_specs + [vmem] * (len(tests) + 2)
    return pl.pallas_call(
        functools.partial(chunk_kernel, distances, places, first, last, side, scale),
        out_shape=out_shape,
        in_specs=in_specs,
        out_specs=[vmem] * len(out_shape),
        scratch_shapes=[
            pltpu.VMEM((height, channels), jnp.bfloat16),
            pltpu.VMEM((height, channels), jnp.bfloat16),
            pltpu.VMEM((blocks, height, 128), jnp.float32),
            pltpu.VMEM((blocks, height, 128), jnp.float32),
            pltpu.VMEM((blocks, height, 128), jnp.float32),
        ],
        compiler_params=pltpu.CompilerParams(vmem_limit_bytes=24 * 1024 * 1024),
        cost_estimate=pl.CostEstimate(
            flops=4 * blocks * 128 * height * channels, bytes_accessed=0, transcendentals=0
        ),
        name="chunk_scores",
    )(*args)


def across(x, distance):
    size = lax.axis_size("rows")
    return lax.ppermute(x, "rows", [(i, i ^ distance) for i in range(size)])


def gather_tests(own):
    size, height = lax.axis_size("rows"), own.shape[0]
    held = {0: own}
    other = across(own, 1)
    if size == 16:
        later, other = lax.optimization_barrier((own, other))
        held[8] = across(own, 8)
        held[4] = across(later, 4)
        held[2] = across(later, 2)
        held[6] = across(later, 6)
        held[14] = across(held[8], 6)
        held[12] = across(held[8], 4)
        held[10] = across(held[8], 2)
        groups = [[0, 2, 4, 6], [8, 10, 12, 14]]
    else:
        bit = 2
        while bit < size:
            for known in list(held):
                held[known ^ bit] = across(held[known], bit)
            bit *= 2
        groups = [list(range(i, i + 2 * CHUNK, 2)) for i in range(0, size, 2 * CHUNK)]
    return held, other, groups


def body(train_act, train_grad, test_act, test_grad, ckpt_weights, owner_ids):
    tr_dev, side, channels = train_act.shape[1], train_act.shape[2], train_act.shape[4]
    size = lax.axis_size("rows")
    act = train_act[0].transpose(1, 2, 0, 3).reshape(-1, channels)
    grad = train_grad[0].transpose(1, 2, 0, 3).reshape(-1, channels)
    ids = owner_ids.reshape(1, tr_dev)
    held, other, groups = gather_tests(pack_test(test_act[0, 0], test_grad[0, 0]))

    me = lax.axis_index("rows").reshape(1)
    scale = 1.0 / (3.0 * side * side * channels)
    scores, came, sent_on = None, {1: other}, {}
    for k in range(len(groups) + 1):
        last, group = k == len(groups), groups[k] if k < len(groups) else []
        came, sent_on = came | sent_on, {}
        distances, arrays = group + list(came), [held[d] for d in group] + list(came.values())
        late = group[1:] if k else []
        if late:
            *sent, scores = lax.optimization_barrier((*[held[d] for d in late], scores))
        sent = dict(zip(late, sent)) if late else {}
        came = {}
        if k:
            sent_on = {d ^ 1: across(sent.get(d, held[d]), 1) for d in group}
        places = [(test, 0) for test in range(len(arrays))]
        done = chunk_scores(
            distances, places, last, side, size, scale, me, ckpt_weights, ids, scores, arrays, act, grad
        )
        scores = done[0]
        if k == 0:
            *sent, scores = lax.optimization_barrier((*[held[d] for d in group[1:]], scores))
            sent_on = {d ^ 1: across(x, 1) for d, x in zip(group[1:], sent)}
    scores, packed = done
    received = lax.all_to_all(packed, "rows", split_axis=0, concat_axis=0, tiled=True)
    return scores[:, :tr_dev].T, jnp.sum(received, axis=0, keepdims=True)


def solution(mesh):
    placed = (
        P(None, ("grp", "rows"), None, None, None),
        P(None, ("grp", "rows"), None, None, None),
        P(None, ("grp", "rows"), None, None, None),
        P(None, ("grp", "rows"), None, None, None),
        P(),
        P(("grp", "rows"), None),
    )
    return jax.shard_map(
        body,
        mesh=mesh,
        in_specs=placed,
        out_specs=(P(("grp", "rows"), None), P(("grp", "rows"), None)),
        check_vma=False,
    )
```
